32 devices in a mesh: dp: 4 (over x, core), hidden: 4 (over z), mp: 2 (over y).
Axes of the slice: x: 2, y: 2, z: 4, core: 2. Of those that a mesh axis runs over, the one named last changes fastest.
Arguments:
- activations: bfloat16 [2048, 26624], P('dp', 'hidden'), may hold values from -6 to 6
- weight: bfloat16 [26624, 8192], P('hidden', 'mp'), may hold values from -0.0390625 to 0.0390625
- out_grad: bfloat16 [2048, 8192], P(('dp', 'hidden'), 'mp'), may hold values from -0.3125 to 0.3125
- momentum: float32 [4, 6656, 8192], P('dp', 'hidden', 'mp'), may hold values from -6 to 6
Outputs:
- output: bfloat16 [2048, 8192], P(('dp', 'hidden'), 'mp')
- new_momentum: float32 [4, 6656, 8192], P('dp', 'hidden', 'mp')
- new_weight: bfloat16 [4, 6656, 8192], P('dp', 'hidden', 'mp')
The draws below stay inside these ranges and needn't reach their ends.
All inputs are finite; a program needn't handle non-finite values.
Results may differ from the reference program's by a relative error of at most 0.015.
Values may be sent and summed in bfloat16 or wider, within the bound.
A program may use at most 256 MiB of HBM per device.

```python
import jax
import jax.numpy as jnp
from jax import lax

D = 8192
HID = 26624
TOK_DEV = 512
GROUPS = 4
HID_BLOCKS = 4
TOKENS = 2048
SLAB = 1664
N_DP = 4


def levels(own_key, shape, pieces, low, top_value):
    def one(position, shards_of):
        steps = jax.random.uniform(jax.random.fold_in(jax.random.fold_in(own_key, 6), position), (shards_of,), jnp.float32, low / len(pieces), top_value / len(pieces))
        return jnp.repeat(jnp.exp(steps), shape[position] // shards_of).reshape((-1,) + (1,) * (len(shape) - position - 1))

    loudness = one(*pieces[0])
    for cut in pieces[1:]:
        loudness = loudness * one(*cut)
    return loudness


def scatter_about(key, shape, width, bound, pieces=(), held_as=jnp.bfloat16):
    factor_of = levels(key, shape, pieces, -0.22, 0.18) if pieces else 1.0
    drawn = jax.random.normal(key, shape, jnp.float32) * width * factor_of
    return jnp.minimum(jnp.maximum(drawn, -bound), bound).astype(held_as)


def setup_inputs(seed: int = 0) -> dict:
    keys = jax.random.split(jax.random.key(seed), 5)
    activations = scatter_about(keys[0], (TOKENS, HID), 1.0, 6.0, ((0, 4), (1, 4)))
    weight = scatter_about(keys[1], (HID, D), HID ** -0.5, 0.0390625, ((0, 4), (1, 2)))
    out_grad = scatter_about(keys[2], (TOKENS, D), ((TOK_DEV * N_DP) ** -0.5), 0.3125, ((0, 16), (1, 2)))
    momentum = scatter_about(keys[3], (GROUPS, HID // GROUPS, D), 1.0, 6.0, ((0, 4), (1, 4), (2, 2)), jnp.float32)
    return {"activations": activations, "weight": weight, "out_grad": out_grad, "momentum": momentum}


momentum_decay = 0.9
step_size = 0.05


def stack_slabs(matrix):
    shaped = matrix.reshape(HID_BLOCKS, GROUPS, SLAB, D)
    return jnp.transpose(shaped, (1, 0, 2, 3)).reshape(GROUPS, HID // GROUPS, D)


def reference(activations, weight, out_grad, momentum):
    output = jnp.dot(activations, weight, preferred_element_type=jnp.float32).astype(jnp.bfloat16)

    def add_group(group, running):
        first_row = (group * TOK_DEV).astype(jnp.int32)
        act_rows = lax.dynamic_slice_in_dim(activations, first_row, TOK_DEV, 0)
        grad_rows = lax.dynamic_slice_in_dim(out_grad, first_row, TOK_DEV, 0)
        partial_value = lax.dot_general(act_rows, grad_rows, (((0,), (0,)), ((), ())), preferred_element_type=jnp.float32)
        return running + partial_value.astype(jnp.bfloat16).astype(jnp.float32)

    gradient = lax.fori_loop(0, GROUPS, add_group, jnp.zeros((HID, D), jnp.float32))
    new_momentum = momentum_decay * momentum + stack_slabs(gradient)
    new_weight = (stack_slabs(weight).astype(jnp.float32) - step_size * new_momentum).astype(jnp.bfloat16)
    return output, new_momentum, new_weight
```

```python
import functools

import jax
import jax.numpy as jnp
from jax import lax
from jax.sharding import PartitionSpec as P

momentum_decay = 0.9
step_size = 0.05
parts = 2


def on_device(n_dp, n_hidden, activations, weight, out_grad, momentum):
    slab_rows = momentum.shape[1]
    me = lax.axis_index("dp")
    rows = out_grad.shape[0] // parts

    group_grad = [
        lax.all_gather(out_grad[h * rows:(h + 1) * rows], "hidden", axis=0, tiled=True)
        for h in range(parts)
    ]

    def columns_for(target):
        block = lax.dynamic_slice_in_dim(activations, target * slab_rows, slab_rows, 1)
        block = block.reshape(n_hidden, parts, rows, slab_rows)
        return block.transpose(1, 0, 2, 3).reshape(parts, n_hidden * rows, slab_rows)

    acts = {}
    for shift in range(n_dp // 2):
        for flip in range(2):
            if shift == 0 and flip == 0:
                acts[shift, flip] = columns_for(me)
                continue
            target = lax.rem((me ^ flip) + 2 * shift, n_dp)
            acts[shift, flip] = lax.ppermute(
                columns_for(target),
                "dp",
                [(j, ((j ^ flip) + 2 * shift) % n_dp) for j in range(n_dp)],
            )

    summed = lax.psum_scatter(
        jnp.dot(activations, weight, preferred_element_type=jnp.float32).astype(jnp.bfloat16),
        "hidden",
        scatter_dimension=0,
        tiled=True,
    )

    swap = [(j, j ^ 1) for j in range(n_dp)]
    total = momentum_decay * momentum[0]
    for shift in range(n_dp // 2):
        for h in range(parts):
            near = group_grad[h]
            if shift:
                near = lax.ppermute(
                    near, "dp", [(j, (j + 2 * shift) % n_dp) for j in range(n_dp)]
                )
                near, total = lax.optimization_barrier((near, total))
            far = lax.ppermute(near, "dp", swap)
            total = total + lax.dot_general(
                jnp.concatenate([acts[shift, 0][h], acts[shift, 1][h]], axis=0),
                jnp.concatenate([near, far], axis=0),
                (((0,), (0,)), ((), ())),
                preferred_element_type=jnp.float32,
            )
    new_momentum = total[None]
    own_rows = lax.dynamic_slice_in_dim(weight, me * slab_rows, slab_rows, 0)
    new_weight = (own_rows.astype(jnp.float32)[None] - step_size * new_momentum).astype(
        jnp.bfloat16
    )
    return (summed, new_momentum, new_weight)


def solution(mesh):
    placed = (
        P("dp", "hidden"),
        P("hidden", "mp"),
        P(("dp", "hidden"), "mp"),
        P("dp", "hidden", "mp"),
    )
    return jax.shard_map(
        functools.partial(on_device, mesh.shape["dp"], mesh.shape["hidden"]),
        mesh=mesh,
        in_specs=placed,
        out_specs=(P(("dp", "hidden"), "mp"), P("dp", "hidden", "mp"), P("dp", "hidden", "mp")),
        check_vma=False,
    )
```

```python
import functools

import jax
import jax.numpy as jnp
from jax import lax
from jax.sharding import PartitionSpec as P

momentum_decay = 0.9
step_size = 0.05
parts = 2


def on_device(n_dp, n_hidden, activations, weight, out_grad, momentum):
    slab_rows = momentum.shape[1]
    me = lax.axis_index("dp")
    rows = out_grad.shape[0] // parts

    group_grad = [
        lax.all_gather(out_grad[h * rows:(h + 1) * rows], "hidden", axis=0, tiled=True)
        for h in range(parts)
    ]

    def columns_for(target):
        block = lax.dynamic_slice_in_dim(activations, target * slab_rows, slab_rows, 1)
        block = block.reshape(n_hidden, parts, rows, slab_rows)
        return block.transpose(1, 0, 2, 3).reshape(parts, n_hidden * rows, slab_rows)

    blocks = {
        (shift, flip): columns_for(lax.rem((me ^ flip) + 2 * shift, n_dp))
        for shift in range(n_dp // 2)
        for flip in range(2)
    }
    blocks, act_rows = lax.optimization_barrier((blocks, activations))
    acts = {
        (shift, flip): lax.ppermute(
            block, "dp", [(j, ((j ^ flip) + 2 * shift) % n_dp) for j in range(n_dp)]
        )
        if shift or flip
        else block
        for (shift, flip), block in blocks.items()
    }

    product = jnp.dot(act_rows, weight, preferred_element_type=jnp.float32).astype(jnp.bfloat16)
    summed = lax.psum_scatter(product, "hidden", scatter_dimension=0, tiled=True)
    _, acts, group_grad[0] = lax.optimization_barrier((product, acts, group_grad[0]))

    swap = [(j, j ^ 1) for j in range(n_dp)]
    total = momentum_decay * momentum[0]
    for shift in range(n_dp // 2):
        lefts, rights = [], []
        for h in range(parts):
            near = group_grad[h]
            if shift:
                near = lax.ppermute(
                    near, "dp", [(j, (j + 2 * shift) % n_dp) for j in range(n_dp)]
                )
                if h == 0:
                    near, total = lax.optimization_barrier((near, total))
            lefts += [acts[shift, 0][h], acts[shift, 1][h]]
            rights += [near, lax.ppermute(near, "dp", swap)]
        if shift + 1 == n_dp // 2:
            summed, total = lax.optimization_barrier((summed, total))
        total = total + lax.dot_general(
            jnp.concatenate(lefts, axis=0),
            jnp.concatenate(rights, axis=0),
            (((0,), (0,)), ((), ())),
            preferred_element_type=jnp.float32,
        )
    new_momentum = total[None]
    own_rows = lax.dynamic_slice_in_dim(weight, me * slab_rows, slab_rows, 0)
    new_weight = (own_rows.astype(jnp.float32)[None] - step_size * new_momentum).astype(
        jnp.bfloat16
    )
    return (summed, new_momentum, new_weight)


def solution(mesh):
    placed = (
        P("dp", "hidden"),
        P("hidden", "mp"),
        P(("dp", "hidden"), "mp"),
        P("dp", "hidden", "mp"),
    )
    return jax.shard_map(
        functools.partial(on_device, mesh.shape["dp"], mesh.shape["hidden"]),
        mesh=mesh,
        in_specs=placed,
        out_specs=(P(("dp", "hidden"), "mp"), P("dp", "hidden", "mp"), P("dp", "hidden", "mp")),
        check_vma=False,
    )
```
